32 devices in a mesh: leaf: 32 (over z, y, x, core).
Axes of the slice: x: 2, y: 2, z: 4, core: 2. Of those that a mesh axis runs over, the one named last changes fastest.
Arguments:
- charges: bfloat16 [16, 262144], P(None, 'leaf'), may hold values from -6 to 6
- points: bfloat16 [3, 262144], P(None, 'leaf'), may hold values from 0 to 1
- leaf_basis: bfloat16 [256, 1024, 128], P('leaf'), may hold values from -0.1875 to 0.1875
- transfer: float32 [4, 2, 128, 128], replicated, may hold values from -0.375 to 0.375
- coupling: float32 [4, 3, 128, 128], replicated, may hold values from -0.5 to 0.5
- near_list: int32 [256, 5], P('leaf'), may hold values from 0 to 255, as said below
- couple_flags: int32 [32, 4, 3], P('leaf'), may hold values from 0 to 1, as said below
Outputs:
- potential: bfloat16 [16, 262144], P(None, 'leaf')
The draws below stay inside these ranges and needn't reach their ends.
Inputs may be any that keep to these rules, and one draw needn't show every extreme that they name: `near_list`: entries of a row are distinct leaves within 32 of the row's leaf i; the first is i itself and the second lies exactly 32 away from i. `couple_flags`: at level t the flags are equal for all clusters c with equal c // 2^t.
All inputs are finite; a program needn't handle non-finite values.
Results may differ from the reference program's by a relative error of at most 0.0049.
Values may be sent and summed in bfloat16 or wider, within the bound.
A program may use at most 64 MiB of HBM per device.

```python
import math
import jax
import jax.numpy as jnp
from jax import lax

LEAF = 1024
RANK = 128
RHS = 16
NB = 5
LEVELS = 4
LEAVES_DEV = 8
RADIUS = 32
CLUSTERS = 32
LEAVES = 256
ROWS = 262144


def draw_near_list(key, part):
    key = jax.random.fold_in(key, 11)
    span = 2 * RADIUS + 1
    offsets = jnp.arange(-RADIUS, RADIUS + 1, dtype=jnp.int32)
    leaf_ids = jnp.arange(LEAVES, dtype=jnp.int32)[:, None]
    candidates = leaf_ids + offsets[None, :]
    inside = (candidates >= 0) & (candidates < LEAVES)
    far_leaf = jnp.where(leaf_ids[:, 0] + RADIUS < LEAVES, leaf_ids[:, 0] + RADIUS, leaf_ids[:, 0] - RADIUS)
    scores = jax.random.randint(key, (LEAVES, span), 0, 2 ** 20) * span + jnp.arange(span, dtype=jnp.int32)[None, :]
    usable = inside & (candidates != leaf_ids) & (candidates != far_leaf[:, None])
    scores = jnp.where(usable, scores, -1)
    unused, chosen_cols = lax.top_k(scores, NB - 2)
    chosen = jnp.take_along_axis(candidates, chosen_cols, axis=1)
    return jnp.concatenate([leaf_ids, far_leaf[:, None], chosen], axis=1).astype(jnp.int32)


def draw_couple_flags(key, part):
    key = jax.random.fold_in(key, 12)
    random_bits = jax.random.randint(key, (CLUSTERS, LEVELS, 3), 0, 2)
    node_ids = jnp.arange(CLUSTERS, dtype=jnp.int32)
    per_level = [random_bits[node_ids // 2 ** t * 2 ** t, t] for t in range(LEVELS)]
    return jnp.stack(per_level, axis=1).astype(jnp.int32)


def level_of(rng, extent, shards, least, largest):
    def one(axis_at, blocks):
        draws = jax.random.uniform(jax.random.fold_in(jax.random.fold_in(rng, 6), axis_at), (blocks,), jnp.float32, least / len(shards), largest / len(shards))
        return jnp.repeat(jnp.exp(draws), extent[axis_at] // blocks).reshape((-1,) + (1,) * (len(extent) - axis_at - 1))

    loudness = one(*shards[0])
    for cut in shards[1:]:
        loudness = loudness * one(*cut)
    return loudness


def normal_values(stream_key, extent, deviation, bound, cuts=(), kind=jnp.bfloat16):
    entries = jax.random.normal(stream_key, extent, jnp.float32) * deviation
    if len(cuts) > 0:
        entries = level_of(stream_key, extent, cuts, -0.22, 0.18) * entries
    return jnp.clip(entries, min=-bound, max=bound).astype(kind)


def setup_inputs(seed: int = 0) -> dict:
    key_list = jax.random.split(jax.random.key(seed), 8)
    charges = normal_values(key_list[0], (RHS, ROWS), 1.0, 6.0, ((1, 32),))
    points = jnp.clip(1.0 * jax.random.uniform(key_list[1], (3, ROWS), jnp.float32) ** level_of(key_list[1], (3, ROWS), ((1, 32),), -0.2, 0.2), 0.0, 1.0).astype(jnp.bfloat16)
    leaf_basis = normal_values(key_list[2], (LEAVES, LEAF, RANK), LEAF ** -0.5, 0.1875, ((0, 32),))
    transfer = normal_values(key_list[3], (LEVELS, 2, RANK, RANK), (2 * RANK) ** -0.5, 0.375, (), jnp.float32)
    coupling = normal_values(key_list[4], (LEVELS, 3, RANK, RANK), RANK ** -0.5, 0.5, (), jnp.float32)
    near_list = draw_near_list(jax.random.fold_in(key_list[7], 71), 0)
    couple_flags = draw_couple_flags(jax.random.fold_in(key_list[7], 71), 0)
    return dict(charges=charges, points=points, leaf_basis=leaf_basis, transfer=transfer, coupling=coupling, near_list=near_list, couple_flags=couple_flags)


smoothing_sq = 0.01

def positions(raw, leaf_num, leaf_step):
    coords = raw.astype(jnp.float32)
    return jnp.stack([coords[0] + leaf_num * leaf_step, coords[1], coords[2]], axis=0)

def kernel_block(src_pos, tgt_pos):
    diff_x = src_pos[0][:, None] - tgt_pos[0][None, :]
    diff_y = src_pos[1][:, None] - tgt_pos[1][None, :]
    diff_z = src_pos[2][:, None] - tgt_pos[2][None, :]
    dist_sq = diff_x * diff_x + diff_y * diff_y + diff_z * diff_z
    return lax.rsqrt(dist_sq + smoothing_sq).astype(jnp.bfloat16)

def reference(charges, points, leaf_basis, transfer, coupling, near_list, couple_flags):
    highest = lax.Precision.HIGHEST
    cluster_rows = LEAVES_DEV * LEAF
    leaf_step = 1.0 / (2.0 * RADIUS)

    def near_leaf(i):
        tgt_pos = positions(lax.dynamic_slice(points, (jnp.int32(0), i * LEAF), (3, LEAF)), i.astype(jnp.float32), leaf_step)
        near_sum = jnp.zeros((RHS, LEAF), jnp.float32)
        for k in range(NB):
            j = near_list[i, k].astype(jnp.int32)
            src_pos = positions(lax.dynamic_slice(points, (jnp.int32(0), j * LEAF), (3, LEAF)), j.astype(jnp.float32), leaf_step)
            src_vals = lax.dynamic_slice(charges, (jnp.int32(0), j * LEAF), (RHS, LEAF))
            near_sum = near_sum + jnp.dot(src_vals, kernel_block(src_pos, tgt_pos), preferred_element_type=jnp.float32)
        return near_sum
    near_field = lax.map(near_leaf, jnp.arange(LEAVES, dtype=jnp.int32))
    near_field = jnp.transpose(near_field, (1, 0, 2)).reshape(RHS, ROWS)

    def cluster_basis(c):
        return lax.dynamic_slice_in_dim(leaf_basis, c * LEAVES_DEV, LEAVES_DEV, 0).reshape(cluster_rows, RANK)

    def upward_leaf(c):
        src_vals = lax.dynamic_slice(charges, (jnp.int32(0), c * cluster_rows), (RHS, cluster_rows))
        return jnp.dot(src_vals, cluster_basis(c), preferred_element_type=jnp.float32)
    level_coef = lax.map(upward_leaf, jnp.arange(CLUSTERS, dtype=jnp.int32))
    coupled_levels = []
    for t in range(LEVELS):
        count = level_coef.shape[0]
        node_ids = jnp.arange(count, dtype=jnp.int32)
        coupled = jnp.zeros((count, RHS, RANK), jnp.float32)
        for m in range(1, 4):
            partner = level_coef[jnp.bitwise_xor(node_ids, m)]
            flag_vals = couple_flags[node_ids * 2 ** t, t, m - 1].astype(jnp.float32)
            product = jnp.einsum('nrk,kl->nrl', partner, coupling[t, m - 1], precision=highest)
            coupled = coupled + flag_vals[:, None, None] * product
        coupled_levels.append(coupled)
        if t + 1 < LEVELS:
            level_coef = jnp.einsum('nrk,kl->nrl', level_coef[0::2], transfer[t, 0], precision=highest) + jnp.einsum('nrk,kl->nrl', level_coef[1::2], transfer[t, 1], precision=highest)
    local_coef = coupled_levels[-1]
    for t in range(LEVELS - 1, 0, -1):
        down_left = jnp.einsum('nrl,kl->nrk', local_coef, transfer[t - 1, 0], precision=highest)
        down_right = jnp.einsum('nrl,kl->nrk', local_coef, transfer[t - 1, 1], precision=highest)
        count = local_coef.shape[0]
        spread = jnp.stack([down_left, down_right], axis=1).reshape(2 * count, RHS, RANK)
        local_coef = coupled_levels[t - 1] + spread
    local_bf = local_coef.astype(jnp.bfloat16)

    def far_leaf(c):
        return lax.dot_general(local_bf[c], cluster_basis(c), (((1,), (1,)), ((), ())), preferred_element_type=jnp.float32)
    far_field = lax.map(far_leaf, jnp.arange(CLUSTERS, dtype=jnp.int32))
    far_field = jnp.transpose(far_field, (1, 0, 2)).reshape(RHS, ROWS)
    near_scale = 1.0 / math.sqrt(NB * LEAF)
    return (near_field * near_scale + far_field).astype(jnp.bfloat16)
```

```python
import functools
import math

import jax
import jax.numpy as jnp
from jax import lax
from jax.experimental import pallas as pl
from jax.experimental.pallas import tpu as pltpu
from jax.sharding import PartitionSpec as P

smoothing_sq = 0.01
reach = 4
tile = 256
f32 = jnp.float32
bf16 = jnp.bfloat16
MESH = pl.DeviceIdType.MESH


def split3(v):
    hi = v.astype(bf16).astype(f32)
    rest = v - hi
    mid = rest.astype(bf16).astype(f32)
    return hi, mid, rest - mid


def near_kernel(n, leaves, neighbours, near_ref, charges_ref, points_ref, out_ref, win, pos, send_sem, recv_sem):
    me = lax.axis_index("leaf")
    core = me % 2
    sibling = me + 1 - 2 * core
    rows = out_ref.shape[-1]
    leaf_step = 1.0 / (2.0 * reach * leaves)

    def each(off, body):
        @pl.when((me + off >= 0) & (me + off < n))
        def _():
            body()

    barrier = pltpu.get_barrier_semaphore()
    pl.semaphore_signal(barrier, inc=1, device_id=(sibling,), device_id_type=MESH)
    for off in (-4, -2, 2, 4):
        each(off, lambda: pl.semaphore_signal(barrier, inc=1, device_id=(me + off,), device_id_type=MESH))

    for l in range(leaves):
        win[reach, l] = charges_ref[:, l * rows:(l + 1) * rows]
    for b in range(points_ref.shape[0]):
        win[reach, leaves + b] = points_ref[b]

    peers = 1
    for off in (-4, -2, 2, 4):
        peers = peers + jnp.where((me + off >= 0) & (me + off < n), 1, 0)
    pl.semaphore_wait(barrier, peers)

    def copy(src_slot, dst_slot, sem, target):
        return pltpu.make_async_remote_copy(
            src_ref=win.at[src_slot],
            dst_ref=win.at[dst_slot],
            send_sem=send_sem.at[sem],
            recv_sem=recv_sem.at[sem],
            device_id=(target,),
            device_id_type=MESH,
        )

    direct = {off: copy(reach, reach - off, i, me + off) for i, off in enumerate((4, -4, 2, -2))}
    received = {off: copy(reach, reach + off, i, me - off) for i, off in enumerate((-4, 4, -2, 2))}
    to_sib = [(copy(reach, reach - 1, 4, sibling), core == 0), (copy(reach, reach + 1, 4, sibling), core == 1)]
    from_sib = [(copy(reach, reach + 1, 4, sibling), core == 0), (copy(reach, reach - 1, 4, sibling), core == 1)]

    def when(cond, body):
        @pl.when(cond)
        def _():
            body()

    for off in (4, -4, 2, -2):
        each(off, lambda: direct[off].start())
    for c, cond in to_sib:
        when(cond, lambda: c.start())

    forwards = [
        (4, 3, 5, 0), (-4, -3, 5, 1),
        (2, 1, 6, 0), (2, 3, 6, 1),
        (-2, -3, 7, 0), (-2, -1, 7, 1),
    ]

    def fwd(entry, act, arriving):
        held, there, sem, sender = entry
        if arriving:
            valid = (me + there >= 0) & (me + there < n) & (core == 1 - sender)
        else:
            valid = (me + held >= 0) & (me + held < n) & (core == sender)
        c = copy(reach + held, reach + there, sem, sibling)
        when(valid, lambda: act(c))

    def to_float(slot):
        for b in range(points_ref.shape[0]):
            pos[slot, b * 16:(b + 1) * 16, :] = win[slot, leaves + b].astype(f32)

    to_float(reach)
    ones = jnp.ones((1, rows), f32)

    def tail(count):
        return jnp.zeros((count, rows), f32)

    def coords(slot, l):
        return [pos[slot, pl.ds(c * leaves + l, 1), :] for c in range(3)]

    def pair(a, offset, source, vals):
        tx, ty, tz = coords(reach, a)
        sx, sy, sz = source
        shift = offset * leaf_step
        norm_t = tx * tx + ty * ty + tz * tz + (shift * shift + smoothing_sq) - (2.0 * shift) * tx
        norm_s = sx * sx + sy * sy + sz * sz
        left = jnp.concatenate([sx, sx, sy, sz, ones, ones, ones, *split3(norm_s), tail(6)], axis=0)
        right = jnp.concatenate(
            [-2.0 * tx, 2.0 * shift * ones, -2.0 * ty, -2.0 * tz, *split3(norm_t), ones, ones, ones, tail(6)], axis=0
        ).astype(bf16)
        left = left.T.astype(bf16)
        sums = []
        for t in range(rows // tile):
            total = jnp.zeros((vals.shape[0], tile), f32)
            for s in range(rows // tile):
                dist_sq = jnp.dot(
                    left[s * tile:(s + 1) * tile, :], right[:, t * tile:(t + 1) * tile], preferred_element_type=f32
                )
                block = lax.rsqrt(dist_sq.astype(bf16))
                total = total + jnp.dot(vals[:, s * tile:(s + 1) * tile], block, preferred_element_type=f32)
            sums.append(total)
        return jnp.concatenate(sums, axis=1)

    def own_leaf(a, carry):
        out_ref[a] = pair(a, 0.0, coords(reach, a), win[reach, a])
        return carry

    lax.fori_loop(0, leaves, own_leaf, 0)

    each(4, lambda: received[4].wait_recv())
    each(-4, lambda: received[-4].wait_recv())
    for entry in forwards[:2]:
        fwd(entry, lambda c: c.start(), False)
    to_float(0)
    to_float(2 * reach)

    def far_leaf(a, carry):
        ahead = near_ref[a, 1] > me * leaves + a
        source = [jnp.where(ahead, x, y) for x, y in zip(coords(2 * reach, a), coords(0, a))]
        vals = jnp.where(ahead, win[2 * reach, a], win[0, a])
        offset = jnp.where(ahead, 1.0, -1.0) * (reach * leaves)
        out_ref[a] += pair(a, offset, source, vals)
        return carry

    lax.fori_loop(0, leaves // 2, far_leaf, 0)
    each(2, lambda: received[2].wait_recv())
    each(-2, lambda: received[-2].wait_recv())
    for entry in forwards[2:]:
        fwd(entry, lambda c: c.start(), False)
    lax.fori_loop(leaves // 2, leaves, far_leaf, 0)

    for c, cond in from_sib:
        when(cond, lambda: c.wait_recv())
    for entry in forwards:
        fwd(entry, lambda c: c.wait_recv(), True)
    for slot in range(1, 2 * reach):
        if slot != reach:
            to_float(slot)

    def other(step, carry):
        a = step // (neighbours - 2)
        k = step % (neighbours - 2) + 2
        j = near_ref[a, k]
        slot = jnp.clip((j >> int(math.log2(leaves))) - me + reach, 0, 2 * reach)
        l = j & (leaves - 1)
        offset = (j - me * leaves - a).astype(f32)
        out_ref[a] += pair(a, offset, coords(slot, l), win[slot, l])
        return carry

    lax.fori_loop(0, leaves * (neighbours - 2), other, 0)

    for off in (4, -4, 2, -2):
        each(off, lambda: direct[off].wait_send())
    for c, cond in to_sib:
        when(cond, lambda: c.wait_send())
    for entry in forwards:
        fwd(entry, lambda c: c.wait_send(), False)


def dot3(a, b, transposed=False):
    dims = (((1,), (1 if transposed else 0,)), ((), ()))
    a_hi = a.astype(bf16)
    b_hi = b.astype(bf16)
    a_lo = (a - a_hi.astype(f32)).astype(bf16)
    b_lo = (b - b_hi.astype(f32)).astype(bf16)

    def one(x, y):
        return lax.dot_general(x, y, dims, preferred_element_type=f32)

    return one(a_hi, b_hi) + (one(a_lo, b_hi) + one(a_hi, b_lo))


def tree_kernel(near_scale, flags_ref, coef_ref, transfer_ref, coupling_ref, basis_ref, near_ref, out_ref, up0, up1, up2, up3):
    levels = transfer_ref.shape[0]
    group, rhs, rank = coef_ref.shape
    place = lax.axis_index("leaf") % group
    ups = (up0, up1, up2, up3)
    up0[...] = coef_ref[...]
    for t in range(levels - 1):
        count = group >> (t + 1)
        vals = ups[t][...].reshape(count, 2, rhs, rank)
        merged = dot3(vals[:, 0].reshape(count * rhs, rank), transfer_ref[t, 0]) + dot3(
            vals[:, 1].reshape(count * rhs, rank), transfer_ref[t, 1]
        )
        ups[t + 1][...] = merged.reshape(count, rhs, rank)
    coupled = []
    for t in range(levels):
        total = jnp.zeros((rhs, rank), f32)
        for m in range(1, 4):
            flag = flags_ref[0, t, m - 1].astype(f32)
            total = total + flag * dot3(ups[t][(place >> t) ^ m], coupling_ref[t, m - 1])
        coupled.append(total)
    coef = coupled[-1]
    for t in range(levels - 1, 0, -1):
        side = (place >> (t - 1)) & 1
        coef = coupled[t - 1] + dot3(coef, transfer_ref[t - 1, side], True)
    coef = coef.astype(bf16)
    leaves, rows = basis_ref.shape[:2]
    for l in range(leaves):
        far = lax.dot_general(coef, basis_ref[l], (((1,), (1,)), ((), ())), preferred_element_type=f32)
        out_ref[:, l * rows:(l + 1) * rows] = (near_ref[l] * near_scale + far).astype(bf16)


def local(n, charges, points, leaf_basis, transfer, coupling, near_list, couple_flags):
    leaves, rows, rank = leaf_basis.shape
    rhs = charges.shape[0]
    levels = transfer.shape[0]
    neighbours = near_list.shape[1]
    basis_rows = leaf_basis.reshape(leaves * rows, rank)
    first = jnp.dot(charges, basis_rows, preferred_element_type=f32)
    group = 2 ** (levels + 1)
    groups = None if n == group else [list(range(g, g + group)) for g in range(0, n, group)]
    coefs = lax.all_gather(first, "leaf", axis_index_groups=groups)
    count = 3 * leaves
    blocks = -(-count // 16)
    packed = jnp.pad(points.reshape(count, rows), ((0, blocks * 16 - count), (0, 0))).reshape(blocks, 16, rows)
    vmem = pl.BlockSpec(memory_space=pltpu.VMEM)
    smem = pl.BlockSpec(memory_space=pltpu.SMEM)
    pairs = leaves * neighbours * rows * rows
    near = pl.pallas_call(
        functools.partial(near_kernel, n, leaves, neighbours),
        out_shape=jax.ShapeDtypeStruct((leaves, rhs, rows), f32),
        in_specs=[smem, vmem, vmem],
        out_specs=vmem,
        scratch_shapes=[
            pltpu.VMEM((2 * reach + 1, leaves + blocks, 16, rows), bf16),
            pltpu.VMEM((2 * reach + 1, blocks * 16, rows), f32),
            pltpu.SemaphoreType.DMA((8,)),
            pltpu.SemaphoreType.DMA((8,)),
        ],
        compiler_params=pltpu.CompilerParams(
            collective_id=0, has_side_effects=True, vmem_limit_bytes=40 * 2**20
        ),
        cost_estimate=pl.CostEstimate(flops=pairs * 2 * 300, bytes_accessed=2**20, transcendentals=pairs),
        name="near_field",
    )(near_list, charges, packed)
    return pl.pallas_call(
        functools.partial(tree_kernel, 1.0 / math.sqrt(neighbours * rows)),
        out_shape=jax.ShapeDtypeStruct((rhs, leaves * rows), bf16),
        in_specs=[smem] + [vmem] * 5,
        out_specs=vmem,
        scratch_shapes=[pltpu.VMEM((group >> t, rhs, rank), f32) for t in range(levels)],
        compiler_params=pltpu.CompilerParams(vmem_limit_bytes=40 * 2**20),
        name="tree_far_field",
    )(couple_flags, coefs, transfer, coupling, leaf_basis, near)


def solution(mesh):
    return jax.shard_map(
        functools.partial(local, mesh.shape["leaf"]),
        mesh=mesh,
        in_specs=(
            P(None, "leaf"),
            P(None, "leaf"),
            P("leaf", None, None),
            P(),
            P(),
            P("leaf", None),
            P("leaf", None, None),
        ),
        out_specs=P(None, "leaf"),
        check_vma=False,
    )
```

```python
import functools
import math

import jax
import jax.numpy as jnp
from jax import lax
from jax.experimental import pallas as pl
from jax.experimental.pallas import tpu as pltpu
from jax.sharding import PartitionSpec as P

smoothing_sq = 0.01
reach = 4
tile = 256
f32 = jnp.float32
bf16 = jnp.bfloat16
MESH = pl.DeviceIdType.MESH


def split3(v):
    hi = v.astype(bf16).astype(f32)
    rest = v - hi
    mid = rest.astype(bf16).astype(f32)
    return hi, mid, rest - mid


def near_kernel(n, leaves, neighbours, near_ref, charges_ref, points_ref, first_ref, out_ref, all_ref, win, pos, coefs, send_sem, recv_sem):
    me = lax.axis_index("leaf")
    core = me % 2
    sibling = me + 1 - 2 * core
    rows = out_ref.shape[-1]
    leaf_step = 1.0 / (2.0 * reach * leaves)

    def each(off, body):
        @pl.when((me + off >= 0) & (me + off < n))
        def _():
            body()

    barrier = pltpu.get_barrier_semaphore()
    group, rhs, rank = coefs.shape
    steps = int(math.log2(group))
    for partner in [sibling] + [me ^ (1 << t) for t in range(3, steps)]:
        pl.semaphore_signal(barrier, inc=1, device_id=(partner,), device_id_type=MESH)
    for off in (-4, -2, 2, 4):
        each(off, lambda: pl.semaphore_signal(barrier, inc=1, device_id=(me + off,), device_id_type=MESH))

    for l in range(leaves):
        win[reach, l] = charges_ref[:, l * rows:(l + 1) * rows]
    for b in range(points_ref.shape[0]):
        win[reach, leaves + b] = points_ref[b]

    peers = 1 + steps - 3
    for off in (-4, -2, 2, 4):
        peers = peers + jnp.where((me + off >= 0) & (me + off < n), 1, 0)
    place = me % group
    coefs[place] = first_ref[...]
    pl.semaphore_wait(barrier, peers)

    def gather(t, incoming=False):
        start = (place >> t) << t
        if incoming:
            start = start ^ (1 << t)
        return pltpu.make_async_remote_copy(
            src_ref=coefs.at[pl.ds(start, 1 << t)],
            dst_ref=coefs.at[pl.ds(start, 1 << t)],
            send_sem=send_sem.at[8 + t],
            recv_sem=recv_sem.at[8 + t],
            device_id=(me ^ (1 << t),),
            device_id_type=MESH,
        )

    def advance(t):
        gather(t, True).wait_recv()
        if t + 1 < steps:
            gather(t + 1).start()

    gather(0).start()

    def copy(src_slot, dst_slot, sem, target):
        return pltpu.make_async_remote_copy(
            src_ref=win.at[src_slot],
            dst_ref=win.at[dst_slot],
            send_sem=send_sem.at[sem],
            recv_sem=recv_sem.at[sem],
            device_id=(target,),
            device_id_type=MESH,
        )

    direct = {off: copy(reach, reach - off, i, me + off) for i, off in enumerate((4, -4, 2, -2))}
    received = {off: copy(reach, reach + off, i, me - off) for i, off in enumerate((-4, 4, -2, 2))}
    to_sib = [(copy(reach, reach - 1, 4, sibling), core == 0), (copy(reach, reach + 1, 4, sibling), core == 1)]
    from_sib = [(copy(reach, reach + 1, 4, sibling), core == 0), (copy(reach, reach - 1, 4, sibling), core == 1)]

    def when(cond, body):
        @pl.when(cond)
        def _():
            body()

    for off in (4, -4, 2, -2):
        each(off, lambda: direct[off].start())
    for c, cond in to_sib:
        when(cond, lambda: c.start())

    forwards = [
        (4, 3, 5, 0), (-4, -3, 5, 1),
        (2, 1, 6, 0), (2, 3, 6, 1),
        (-2, -3, 7, 0), (-2, -1, 7, 1),
    ]

    def fwd(entry, act, arriving):
        held, there, sem, sender = entry
        if arriving:
            valid = (me + there >= 0) & (me + there < n) & (core == 1 - sender)
        else:
            valid = (me + held >= 0) & (me + held < n) & (core == sender)
        c = copy(reach + held, reach + there, sem, sibling)
        when(valid, lambda: act(c))

    def to_float(slot):
        for b in range(points_ref.shape[0]):
            pos[slot, b * 16:(b + 1) * 16, :] = win[slot, leaves + b].astype(f32)

    to_float(reach)
    ones = jnp.ones((1, rows), f32)

    def tail(count):
        return jnp.zeros((count, rows), f32)

    def coords(slot, l):
        return [pos[slot, pl.ds(c * leaves + l, 1), :] for c in range(3)]

    def pair(a, offset, source, vals):
        tx, ty, tz = coords(reach, a)
        sx, sy, sz = source
        shift = offset * leaf_step
        norm_t = tx * tx + ty * ty + tz * tz + (shift * shift + smoothing_sq) - (2.0 * shift) * tx
        norm_s = sx * sx + sy * sy + sz * sz
        right = jnp.concatenate(
            [sx, sx, sy, sz, ones, ones, ones, *split3(norm_s), tail(6)], axis=0
        ).astype(bf16)
        left = jnp.concatenate(
            [-2.0 * tx, 2.0 * shift * ones, -2.0 * ty, -2.0 * tz, *split3(norm_t), ones, ones, ones, tail(6)], axis=0
        )
        left = left.T.astype(bf16)

        def distances(t):
            return jnp.dot(left[t * tile:(t + 1) * tile, :], right, preferred_element_type=f32)

        sums = []
        dist_sq = distances(0)
        for t in range(rows // tile):
            later = distances(t + 1) if t + 1 < rows // tile else None
            block = lax.rsqrt(dist_sq.astype(bf16))
            total = lax.dot_general(block, vals, (((1,), (1,)), ((), ())), preferred_element_type=f32)
            sums.append(total.T)
            dist_sq = later
        return jnp.concatenate(sums, axis=1)

    def own_leaf(a, carry):
        out_ref[a] = pair(a, 0.0, coords(reach, a), win[reach, a])
        return carry

    lax.fori_loop(0, leaves, own_leaf, 0)
    advance(0)

    each(4, lambda: received[4].wait_recv())
    each(-4, lambda: received[-4].wait_recv())
    for entry in forwards[:2]:
        fwd(entry, lambda c: c.start(), False)
    to_float(0)
    to_float(2 * reach)

    def far_leaf(a, carry):
        ahead = near_ref[a, 1] > me * leaves + a
        source = [jnp.where(ahead, x, y) for x, y in zip(coords(2 * reach, a), coords(0, a))]
        vals = jnp.where(ahead, win[2 * reach, a], win[0, a])
        offset = jnp.where(ahead, 1.0, -1.0) * (reach * leaves)
        out_ref[a] += pair(a, offset, source, vals)
        return carry

    lax.fori_loop(0, leaves // 2, far_leaf, 0)
    advance(1)
    each(2, lambda: received[2].wait_recv())
    each(-2, lambda: received[-2].wait_recv())
    for entry in forwards[2:]:
        fwd(entry, lambda c: c.start(), False)
    lax.fori_loop(leaves // 2, leaves, far_leaf, 0)
    advance(2)

    for c, cond in from_sib:
        when(cond, lambda: c.wait_recv())
    for entry in forwards:
        fwd(entry, lambda c: c.wait_recv(), True)
    for slot in range(1, 2 * reach):
        if slot != reach:
            to_float(slot)

    def other(step, carry):
        a = step // (neighbours - 2)
        k = step % (neighbours - 2) + 2
        j = near_ref[a, k]
        slot = jnp.clip((j >> int(math.log2(leaves))) - me + reach, 0, 2 * reach)
        l = j & (leaves - 1)
        offset = (j - me * leaves - a).astype(f32)
        out_ref[a] += pair(a, offset, coords(slot, l), win[slot, l])
        return carry

    half = leaves * (neighbours - 2) // 2
    lax.fori_loop(0, half, other, 0)
    for t in range(3, steps - 1):
        advance(t)
    lax.fori_loop(half, 2 * half, other, 0)
    advance(steps - 1)
    all_ref[...] = coefs[...]
    for t in range(steps):
        gather(t).wait_send()

    for off in (4, -4, 2, -2):
        each(off, lambda: direct[off].wait_send())
    for c, cond in to_sib:
        when(cond, lambda: c.wait_send())
    for entry in forwards:
        fwd(entry, lambda c: c.wait_send(), False)


def dot3(a, b, transposed=False):
    dims = (((1,), (1 if transposed else 0,)), ((), ()))
    a_hi = a.astype(bf16)
    b_hi = b.astype(bf16)
    a_lo = (a - a_hi.astype(f32)).astype(bf16)
    b_lo = (b - b_hi.astype(f32)).astype(bf16)

    def one(x, y):
        return lax.dot_general(x, y, dims, preferred_element_type=f32)

    return one(a_hi, b_hi) + (one(a_lo, b_hi) + one(a_hi, b_lo))


def tree_kernel(near_scale, flags_ref, coef_ref, transfer_ref, coupling_ref, basis_ref, near_ref, out_ref, up0, up1, up2, up3):
    levels = transfer_ref.shape[0]
    group, rhs, rank = coef_ref.shape
    place = lax.axis_index("leaf") % group
    ups = (up0, up1, up2, up3)
    up0[...] = coef_ref[...]
    for t in range(levels - 1):
        count = group >> (t + 1)
        vals = ups[t][...].reshape(count, 2, rhs, rank)
        merged = dot3(vals[:, 0].reshape(count * rhs, rank), transfer_ref[t, 0]) + dot3(
            vals[:, 1].reshape(count * rhs, rank), transfer_ref[t, 1]
        )
        ups[t + 1][...] = merged.reshape(count, rhs, rank)
    coupled = []
    for t in range(levels):
        total = jnp.zeros((rhs, rank), f32)
        for m in range(1, 4):
            flag = flags_ref[0, t, m - 1].astype(f32)
            total = total + flag * dot3(ups[t][(place >> t) ^ m], coupling_ref[t, m - 1])
        coupled.append(total)
    coef = coupled[-1]
    for t in range(levels - 1, 0, -1):
        side = (place >> (t - 1)) & 1
        coef = coupled[t - 1] + dot3(coef, transfer_ref[t - 1, side], True)
    coef = coef.astype(bf16)
    leaves, rows = basis_ref.shape[:2]
    for l in range(leaves):
        far = lax.dot_general(coef, basis_ref[l], (((1,), (1,)), ((), ())), preferred_element_type=f32)
        out_ref[:, l * rows:(l + 1) * rows] = (near_ref[l] * near_scale + far).astype(bf16)


def local(n, charges, points, leaf_basis, transfer, coupling, near_list, couple_flags):
    leaves, rows, rank = leaf_basis.shape
    rhs = charges.shape[0]
    levels = transfer.shape[0]
    neighbours = near_list.shape[1]
    basis_rows = leaf_basis.reshape(leaves * rows, rank)
    first = jnp.dot(charges, basis_rows, preferred_element_type=f32)
    group = 2 ** (levels + 1)
    count = 3 * leaves
    blocks = -(-count // 16)
    packed = jnp.pad(points.reshape(count, rows), ((0, blocks * 16 - count), (0, 0))).reshape(blocks, 16, rows)
    vmem = pl.BlockSpec(memory_space=pltpu.VMEM)
    smem = pl.BlockSpec(memory_space=pltpu.SMEM)
    pairs = leaves * neighbours * rows * rows
    near, coefs = pl.pallas_call(
        functools.partial(near_kernel, n, leaves, neighbours),
        out_shape=(
            jax.ShapeDtypeStruct((leaves, rhs, rows), f32),
            jax.ShapeDtypeStruct((group, rhs, rank), f32),
        ),
        in_specs=[smem, vmem, vmem, vmem],
        out_specs=(vmem, vmem),
        scratch_shapes=[
            pltpu.VMEM((2 * reach + 1, leaves + blocks, 16, rows), bf16),
            pltpu.VMEM((2 * reach + 1, blocks * 16, rows), f32),
            pltpu.VMEM((group, rhs, rank), f32),
            pltpu.SemaphoreType.DMA((8 + levels + 1,)),
            pltpu.SemaphoreType.DMA((8 + levels + 1,)),
        ],
        compiler_params=pltpu.CompilerParams(
            collective_id=0, has_side_effects=True, vmem_limit_bytes=40 * 2**20
        ),
        cost_estimate=pl.CostEstimate(flops=pairs * 2 * 300, bytes_accessed=2**20, transcendentals=pairs),
        name="near_field",
    )(near_list, charges, packed, first)
    return pl.pallas_call(
        functools.partial(tree_kernel, 1.0 / math.sqrt(neighbours * rows)),
        out_shape=jax.ShapeDtypeStruct((rhs, leaves * rows), bf16),
        in_specs=[smem] + [vmem] * 5,
        out_specs=vmem,
        scratch_shapes=[pltpu.VMEM((group >> t, rhs, rank), f32) for t in range(levels)],
        compiler_params=pltpu.CompilerParams(vmem_limit_bytes=40 * 2**20),
        name="tree_far_field",
    )(couple_flags, coefs, transfer, coupling, leaf_basis, near)


def solution(mesh):
    return jax.shard_map(
        functools.partial(local, mesh.shape["leaf"]),
        mesh=mesh,
        in_specs=(
            P(None, "leaf"),
            P(None, "leaf"),
            P("leaf", None, None),
            P(),
            P(),
            P("leaf", None),
            P("leaf", None, None),
        ),
        out_specs=P(None, "leaf"),
        check_vma=False,
    )
```

```python
import functools
import math

import jax
import jax.numpy as jnp
from jax import lax
from jax.experimental import pallas as pl
from jax.experimental.pallas import tpu as pltpu
from jax.sharding import PartitionSpec as P

smoothing_sq = 0.01
reach = 4
tile = 256
f32 = jnp.float32
bf16 = jnp.bfloat16
MESH = pl.DeviceIdType.MESH


def split3(v):
    hi = v.astype(bf16).astype(f32)
    rest = v - hi
    mid = rest.astype(bf16).astype(f32)
    return hi, mid, rest - mid


def dot3(a, b, transposed=False):
    dims = (((1,), (1 if transposed else 0,)), ((), ()))
    a_hi = a.astype(bf16)
    b_hi = b.astype(bf16)
    a_lo = (a - a_hi.astype(f32)).astype(bf16)
    b_lo = (b - b_hi.astype(f32)).astype(bf16)

    def one(x, y):
        return lax.dot_general(x, y, dims, preferred_element_type=f32)

    return one(a_hi, b_hi) + (one(a_lo, b_hi) + one(a_hi, b_lo))


def kernel(
    n, leaves, neighbours, near_ref, flags_ref, charges_ref, points_ref, basis_hbm, transfer_hbm, coupling_hbm,
    out_ref, win, pos, targets, near_sum, basis, transfer, coupling, up0, up1, up2, up3, load_sem, send_sem, recv_sem,
):
    me = lax.axis_index("leaf")
    core = me % 2
    sibling = me + 1 - 2 * core
    rows = basis.shape[1]
    coefs = up0
    loads = [
        pltpu.make_async_copy(src, dst, load_sem.at[i])
        for i, (src, dst) in enumerate(((basis_hbm, basis), (transfer_hbm, transfer), (coupling_hbm, coupling)))
    ]
    for c in loads:
        c.start()
    leaf_step = 1.0 / (2.0 * reach * leaves)

    def each(off, body):
        @pl.when((me + off >= 0) & (me + off < n))
        def _():
            body()

    barrier = pltpu.get_barrier_semaphore()
    group, rhs, rank = coefs.shape
    steps = int(math.log2(group))
    for partner in [sibling] + [me ^ (1 << t) for t in range(3, steps)]:
        pl.semaphore_signal(barrier, inc=1, device_id=(partner,), device_id_type=MESH)
    for off in (-4, -2, 2, 4):
        each(off, lambda: pl.semaphore_signal(barrier, inc=1, device_id=(me + off,), device_id_type=MESH))

    for l in range(leaves):
        win[reach, l] = charges_ref[:, l * rows:(l + 1) * rows]
    for b in range(points_ref.shape[0]):
        win[reach, leaves + b] = points_ref[b]

    peers = 1 + steps - 3
    for off in (-4, -2, 2, 4):
        peers = peers + jnp.where((me + off >= 0) & (me + off < n), 1, 0)
    place = me % group
    pl.semaphore_wait(barrier, peers)

    def gather(t, incoming=False):
        start = (place >> t) << t
        if incoming:
            start = start ^ (1 << t)
        return pltpu.make_async_remote_copy(
            src_ref=coefs.at[pl.ds(start, 1 << t)],
            dst_ref=coefs.at[pl.ds(start, 1 << t)],
            send_sem=send_sem.at[8 + t],
            recv_sem=recv_sem.at[8 + t],
            device_id=(me ^ (1 << t),),
            device_id_type=MESH,
        )

    def advance(t):
        gather(t, True).wait_recv()
        if t + 1 < steps:
            gather(t + 1).start()

    def copy(src_slot, dst_slot, sem, target):
        return pltpu.make_async_remote_copy(
            src_ref=win.at[src_slot],
            dst_ref=win.at[dst_slot],
            send_sem=send_sem.at[sem],
            recv_sem=recv_sem.at[sem],
            device_id=(target,),
            device_id_type=MESH,
        )

    direct = {off: copy(reach, reach - off, i, me + off) for i, off in enumerate((4, -4, 2, -2))}
    received = {off: copy(reach, reach + off, i, me - off) for i, off in enumerate((-4, 4, -2, 2))}
    to_sib = [(copy(reach, reach - 1, 4, sibling), core == 0), (copy(reach, reach + 1, 4, sibling), core == 1)]
    from_sib = [(copy(reach, reach + 1, 4, sibling), core == 0), (copy(reach, reach - 1, 4, sibling), core == 1)]

    def when(cond, body):
        @pl.when(cond)
        def _():
            body()

    for off in (4, -4, 2, -2):
        each(off, lambda: direct[off].start())
    for c, cond in to_sib:
        when(cond, lambda: c.start())

    forwards = [
        (4, 3, 5, 0), (-4, -3, 5, 1),
        (2, 1, 6, 0), (2, 3, 6, 1),
        (-2, -3, 7, 0), (-2, -1, 7, 1),
    ]

    def fwd(entry, act, arriving):
        held, there, sem, sender = entry
        if arriving:
            valid = (me + there >= 0) & (me + there < n) & (core == 1 - sender)
        else:
            valid = (me + held >= 0) & (me + held < n) & (core == sender)
        c = copy(reach + held, reach + there, sem, sibling)
        when(valid, lambda: act(c))

    def to_float(slot):
        for b in range(points_ref.shape[0]):
            pos[slot, b * 16:(b + 1) * 16, :] = win[slot, leaves + b].astype(f32)

    loads[0].wait()
    first = jnp.zeros((rhs, rank), f32)
    for l in range(leaves):
        first = first + jnp.dot(win[reach, l], basis[l], preferred_element_type=f32)
    coefs[place] = first
    gather(0).start()

    to_float(reach)
    ones = jnp.ones((1, rows), f32)

    def tail(count):
        return jnp.zeros((count, rows), f32)

    def coords(slot, l):
        return [pos[slot, pl.ds(c * leaves + l, 1), :] for c in range(3)]

    def target(a, carry):
        tx, ty, tz = coords(reach, a)
        feats = jnp.concatenate(
            [-2.0 * tx, -2.0 * ty, -2.0 * tz, tx, *split3(tx * tx + ty * ty + tz * tz), ones, ones, ones, tail(6)],
            axis=0,
        )
        targets[a] = feats.T.astype(bf16)
        return carry

    lax.fori_loop(0, leaves, target, 0)

    def source_features(offset, source):
        sx, sy, sz = source
        shift = offset * leaf_step
        norm = sx * sx + sy * sy + sz * sz + (shift * shift + smoothing_sq) + (2.0 * shift) * sx
        return jnp.concatenate(
            [sx, sy, sz, (-2.0 * shift) * ones, ones, ones, ones, *split3(norm), tail(6)], axis=0
        ).astype(bf16)

    def near_of(a, sources):
        feats = [source_features(offset, source) for offset, source, vals in sources]
        parts = [(t, k) for t in range(rows // tile) for k in range(len(sources))]

        def distances(t, k):
            return jnp.dot(targets[a, t * tile:(t + 1) * tile, :], feats[k], preferred_element_type=f32)

        sums = []
        total = None
        dist_sq = distances(*parts[0])
        for i, (t, k) in enumerate(parts):
            later = distances(*parts[i + 1]) if i + 1 < len(parts) else None
            block = lax.rsqrt(dist_sq.astype(bf16))
            product = lax.dot_general(block, sources[k][2], (((1,), (1,)), ((), ())), preferred_element_type=f32)
            total = product if k == 0 else total + product
            if k == len(sources) - 1:
                sums.append(total.T)
            dist_sq = later
        return jnp.concatenate(sums, axis=1)

    def own_leaves(pair, carry):
        for a in (2 * pair, 2 * pair + 1):
            near_sum[a] = near_of(a, [(0.0, coords(reach, a), win[reach, a])])
        return carry

    lax.fori_loop(0, leaves // 4, own_leaves, 0)
    advance(0)
    lax.fori_loop(leaves // 4, leaves // 2, own_leaves, 0)
    advance(1)

    each(4, lambda: received[4].wait_recv())
    each(-4, lambda: received[-4].wait_recv())
    for entry in forwards[:2]:
        fwd(entry, lambda c: c.start(), False)
    to_float(0)
    to_float(2 * reach)

    def far_leaves(pair, carry):
        for a in (2 * pair, 2 * pair + 1):
            ahead = near_ref[a, 1] > me * leaves + a
            source = [jnp.where(ahead, x, y) for x, y in zip(coords(2 * reach, a), coords(0, a))]
            vals = jnp.where(ahead, win[2 * reach, a], win[0, a])
            offset = jnp.where(ahead, 1.0, -1.0) * (reach * leaves)
            near_sum[a] += near_of(a, [(offset, source, vals)])
        return carry

    lax.fori_loop(0, leaves // 4, far_leaves, 0)
    advance(2)
    each(2, lambda: received[2].wait_recv())
    each(-2, lambda: received[-2].wait_recv())
    for entry in forwards[2:]:
        fwd(entry, lambda c: c.start(), False)
    lax.fori_loop(leaves // 4, leaves // 2, far_leaves, 0)
    for t in range(3, steps):
        advance(t)

    loads[1].wait()
    loads[2].wait()
    levels = transfer.shape[0]
    ups = (up0, up1, up2, up3)
    for t in range(levels - 1):
        count = group >> (t + 1)
        vals = ups[t][...].reshape(count, 2, rhs, rank)
        merged = dot3(vals[:, 0].reshape(count * rhs, rank), transfer[t, 0]) + dot3(
            vals[:, 1].reshape(count * rhs, rank), transfer[t, 1]
        )
        ups[t + 1][...] = merged.reshape(count, rhs, rank)
    coupled = []
    for t in range(levels):
        total = jnp.zeros((rhs, rank), f32)
        for m in range(1, 4):
            flag = flags_ref[0, t, m - 1].astype(f32)
            total = total + flag * dot3(ups[t][(place >> t) ^ m], coupling[t, m - 1])
        coupled.append(total)
    coef = coupled[-1]
    for t in range(levels - 1, 0, -1):
        side = (place >> (t - 1)) & 1
        coef = coupled[t - 1] + dot3(coef, transfer[t - 1, side], True)
    coef = coef.astype(bf16)
    near_scale = 1.0 / math.sqrt(neighbours * rows)
    for l in range(leaves):
        far = lax.dot_general(coef, basis[l], (((1,), (1,)), ((), ())), preferred_element_type=f32)
        near_sum[l] = near_sum[l] * near_scale + far

    for c, cond in from_sib:
        when(cond, lambda: c.wait_recv())
    for entry in forwards:
        fwd(entry, lambda c: c.wait_recv(), True)
    for slot in range(1, 2 * reach):
        if slot != reach:
            to_float(slot)

    def others(a, carry):
        sources = []
        for k in range(2, neighbours):
            j = near_ref[a, k]
            slot = jnp.clip((j >> int(math.log2(leaves))) - me + reach, 0, 2 * reach)
            l = j & (leaves - 1)
            sources.append(((j - me * leaves - a).astype(f32), coords(slot, l), win[slot, l]))
        total = near_sum[a] + near_of(a, sources) * near_scale
        out_ref[:, pl.ds(pl.multiple_of(a * rows, rows), rows)] = total.astype(bf16)
        return carry

    lax.fori_loop(0, leaves, others, 0)

    for t in range(steps):
        gather(t).wait_send()
    for off in (4, -4, 2, -2):
        each(off, lambda: direct[off].wait_send())
    for c, cond in to_sib:
        when(cond, lambda: c.wait_send())
    for entry in forwards:
        fwd(entry, lambda c: c.wait_send(), False)


def local(n, charges, points, leaf_basis, transfer, coupling, near_list, couple_flags):
    leaves, rows, rank = leaf_basis.shape
    rhs = charges.shape[0]
    levels = transfer.shape[0]
    neighbours = near_list.shape[1]
    group = 2 ** (levels + 1)
    count = 3 * leaves
    blocks = -(-count // 16)
    packed = jnp.pad(points.reshape(count, rows), ((0, blocks * 16 - count), (0, 0))).reshape(blocks, 16, rows)
    vmem = pl.BlockSpec(memory_space=pltpu.VMEM)
    smem = pl.BlockSpec(memory_space=pltpu.SMEM)
    pairs = leaves * neighbours * rows * rows
    hbm = pl.BlockSpec(memory_space=pl.ANY)
    return pl.pallas_call(
        functools.partial(kernel, n, leaves, neighbours),
        out_shape=jax.ShapeDtypeStruct(charges.shape, bf16),
        in_specs=[smem, smem, vmem, vmem, hbm, hbm, hbm],
        out_specs=vmem,
        scratch_shapes=[
            pltpu.VMEM((2 * reach + 1, leaves + blocks, 16, rows), bf16),
            pltpu.VMEM((2 * reach + 1, blocks * 16, rows), f32),
            pltpu.VMEM((leaves, rows, 16), bf16),
            pltpu.VMEM((leaves, rhs, rows), f32),
            pltpu.VMEM(leaf_basis.shape, bf16),
            pltpu.VMEM(transfer.shape, f32),
            pltpu.VMEM(coupling.shape, f32),
            *[pltpu.VMEM((group >> t, rhs, rank), f32) for t in range(levels)],
            pltpu.SemaphoreType.DMA((3,)),
            pltpu.SemaphoreType.DMA((8 + levels + 1,)),
            pltpu.SemaphoreType.DMA((8 + levels + 1,)),
        ],
        compiler_params=pltpu.CompilerParams(
            collective_id=0, has_side_effects=True, vmem_limit_bytes=48 * 2**20
        ),
        cost_estimate=pl.CostEstimate(flops=pairs * 2 * 300, bytes_accessed=2**20, transcendentals=pairs),
        name="h2_matvec",
    )(near_list, couple_flags, charges, packed, leaf_basis, transfer, coupling)


def solution(mesh):
    return jax.shard_map(
        functools.partial(local, mesh.shape["leaf"]),
        mesh=mesh,
        in_specs=(
            P(None, "leaf"),
            P(None, "leaf"),
            P("leaf", None, None),
            P(),
            P(),
            P("leaf", None),
            P("leaf", None, None),
        ),
        out_specs=P(None, "leaf"),
        check_vma=False,
    )
```

```python
import functools
import math

import jax
import jax.numpy as jnp
from jax import lax
from jax.experimental import pallas as pl
from jax.experimental.pallas import tpu as pltpu
from jax.sharding import PartitionSpec as P

smoothing_sq = 0.01
reach = 4
tile = 256
f32 = jnp.float32
bf16 = jnp.bfloat16
MESH = pl.DeviceIdType.MESH


def split3(v):
    hi = v.astype(bf16).astype(f32)
    rest = v - hi
    mid = rest.astype(bf16).astype(f32)
    return hi, mid, rest - mid


def near_kernel(n, leaves, neighbours, near_ref, charges_ref, points_ref, first_ref, out_ref, all_ref, win, pos, targets, coefs, send_sem, recv_sem):
    me = lax.axis_index("leaf")
    core = me % 2
    sibling = me + 1 - 2 * core
    rows = out_ref.shape[-1]
    leaf_step = 1.0 / (2.0 * reach * leaves)

    def each(off, body):
        @pl.when((me + off >= 0) & (me + off < n))
        def _():
            body()

    barrier = pltpu.get_barrier_semaphore()
    group, rhs, rank = coefs.shape
    steps = int(math.log2(group))
    for partner in [sibling] + [me ^ (1 << t) for t in range(3, steps)]:
        pl.semaphore_signal(barrier, inc=1, device_id=(partner,), device_id_type=MESH)
    for off in (-4, -2, 2, 4):
        each(off, lambda: pl.semaphore_signal(barrier, inc=1, device_id=(me + off,), device_id_type=MESH))

    for l in range(leaves):
        win[reach, l] = charges_ref[:, l * rows:(l + 1) * rows]
    for b in range(points_ref.shape[0]):
        win[reach, leaves + b] = points_ref[b]

    peers = 1 + steps - 3
    for off in (-4, -2, 2, 4):
        peers = peers + jnp.where((me + off >= 0) & (me + off < n), 1, 0)
    place = me % group
    coefs[place] = first_ref[...]
    pl.semaphore_wait(barrier, peers)

    def gather(t, incoming=False):
        start = (place >> t) << t
        if incoming:
            start = start ^ (1 << t)
        return pltpu.make_async_remote_copy(
            src_ref=coefs.at[pl.ds(start, 1 << t)],
            dst_ref=coefs.at[pl.ds(start, 1 << t)],
            send_sem=send_sem.at[8 + t],
            recv_sem=recv_sem.at[8 + t],
            device_id=(me ^ (1 << t),),
            device_id_type=MESH,
        )

    def advance(t):
        gather(t, True).wait_recv()
        if t + 1 < steps:
            gather(t + 1).start()

    gather(0).start()

    def copy(src_slot, dst_slot, sem, target):
        return pltpu.make_async_remote_copy(
            src_ref=win.at[src_slot],
            dst_ref=win.at[dst_slot],
            send_sem=send_sem.at[sem],
            recv_sem=recv_sem.at[sem],
            device_id=(target,),
            device_id_type=MESH,
        )

    direct = {off: copy(reach, reach - off, i, me + off) for i, off in enumerate((4, -4, 2, -2))}
    received = {off: copy(reach, reach + off, i, me - off) for i, off in enumerate((-4, 4, -2, 2))}
    to_sib = [(copy(reach, reach - 1, 4, sibling), core == 0), (copy(reach, reach + 1, 4, sibling), core == 1)]
    from_sib = [(copy(reach, reach + 1, 4, sibling), core == 0), (copy(reach, reach - 1, 4, sibling), core == 1)]

    def when(cond, body):
        @pl.when(cond)
        def _():
            body()

    for off in (4, -4, 2, -2):
        each(off, lambda: direct[off].start())
    for c, cond in to_sib:
        when(cond, lambda: c.start())

    forwards = [
        (4, 3, 5, 0), (-4, -3, 5, 1),
        (2, 1, 6, 0), (2, 3, 6, 1),
        (-2, -3, 7, 0), (-2, -1, 7, 1),
    ]

    def fwd(entry, act, arriving):
        held, there, sem, sender = entry
        if arriving:
            valid = (me + there >= 0) & (me + there < n) & (core == 1 - sender)
        else:
            valid = (me + held >= 0) & (me + held < n) & (core == sender)
        c = copy(reach + held, reach + there, sem, sibling)
        when(valid, lambda: act(c))

    def to_float(slot):
        for b in range(points_ref.shape[0]):
            pos[slot, b * 16:(b + 1) * 16, :] = win[slot, leaves + b].astype(f32)

    to_float(reach)
    ones = jnp.ones((1, rows), f32)

    def tail(count):
        return jnp.zeros((count, rows), f32)

    def coords(slot, l):
        return [pos[slot, pl.ds(c * leaves + l, 1), :] for c in range(3)]

    def target(a, carry):
        tx, ty, tz = coords(reach, a)
        feats = jnp.concatenate(
            [-2.0 * tx, -2.0 * ty, -2.0 * tz, tx, *split3(tx * tx + ty * ty + tz * tz), ones, ones, ones, tail(6)],
            axis=0,
        )
        targets[a] = feats.T.astype(bf16)
        return carry

    lax.fori_loop(0, leaves, target, 0)

    def source_features(offset, source):
        sx, sy, sz = source
        shift = offset * leaf_step
        norm = sx * sx + sy * sy + sz * sz + (shift * shift + smoothing_sq) + (2.0 * shift) * sx
        return jnp.concatenate(
            [sx, sy, sz, (-2.0 * shift) * ones, ones, ones, ones, *split3(norm), tail(6)], axis=0
        ).astype(bf16)

    def near_of(a, sources):
        parts = [(s, k) for k in range(len(sources)) for s in range(rows // tile)]
        feats = [source_features(offset, source) for offset, source, vals in sources]

        def distances(s, k):
            return jnp.dot(targets[a], feats[k][:, s * tile:(s + 1) * tile], preferred_element_type=f32)

        total = None
        dist_sq = distances(*parts[0])
        for i, (s, k) in enumerate(parts):
            later = distances(*parts[i + 1]) if i + 1 < len(parts) else None
            block = lax.rsqrt(dist_sq.astype(bf16))
            product = lax.dot_general(
                block, sources[k][2][:, s * tile:(s + 1) * tile], (((1,), (1,)), ((), ())), preferred_element_type=f32
            )
            total = product if total is None else total + product
            dist_sq = later
        return total.T

    def own_leaf(a, carry):
        out_ref[a] = near_of(a, [(0.0, coords(reach, a), win[reach, a])])
        return carry

    lax.fori_loop(0, leaves, own_leaf, 0)
    advance(0)

    each(4, lambda: received[4].wait_recv())
    each(-4, lambda: received[-4].wait_recv())
    for entry in forwards[:2]:
        fwd(entry, lambda c: c.start(), False)
    to_float(0)
    to_float(2 * reach)

    def far_leaf(a, carry):
        ahead = near_ref[a, 1] > me * leaves + a
        source = [jnp.where(ahead, x, y) for x, y in zip(coords(2 * reach, a), coords(0, a))]
        vals = jnp.where(ahead, win[2 * reach, a], win[0, a])
        offset = jnp.where(ahead, 1.0, -1.0) * (reach * leaves)
        out_ref[a] += near_of(a, [(offset, source, vals)])
        return carry

    lax.fori_loop(0, leaves // 2, far_leaf, 0)
    advance(1)
    each(2, lambda: received[2].wait_recv())
    each(-2, lambda: received[-2].wait_recv())
    for entry in forwards[2:]:
        fwd(entry, lambda c: c.start(), False)
    lax.fori_loop(leaves // 2, leaves, far_leaf, 0)
    advance(2)

    for c, cond in from_sib:
        when(cond, lambda: c.wait_recv())
    for entry in forwards:
        fwd(entry, lambda c: c.wait_recv(), True)
    for slot in range(1, 2 * reach):
        if slot != reach:
            to_float(slot)

    def others(a, carry):
        sources = []
        for k in range(2, neighbours):
            j = near_ref[a, k]
            slot = jnp.clip((j >> int(math.log2(leaves))) - me + reach, 0, 2 * reach)
            l = j & (leaves - 1)
            sources.append(((j - me * leaves - a).astype(f32), coords(slot, l), win[slot, l]))
        out_ref[a] += near_of(a, sources)
        return carry

    lax.fori_loop(0, leaves // 2, others, 0)
    for t in range(3, steps - 1):
        advance(t)
    lax.fori_loop(leaves // 2, leaves, others, 0)
    advance(steps - 1)
    all_ref[...] = coefs[...]
    for t in range(steps):
        gather(t).wait_send()

    for off in (4, -4, 2, -2):
        each(off, lambda: direct[off].wait_send())
    for c, cond in to_sib:
        when(cond, lambda: c.wait_send())
    for entry in forwards:
        fwd(entry, lambda c: c.wait_send(), False)


def dot3(a, b, transposed=False):
    dims = (((1,), (1 if transposed else 0,)), ((), ()))
    a_hi = a.astype(bf16)
    b_hi = b.astype(bf16)
    a_lo = (a - a_hi.astype(f32)).astype(bf16)
    b_lo = (b - b_hi.astype(f32)).astype(bf16)

    def one(x, y):
        return lax.dot_general(x, y, dims, preferred_element_type=f32)

    return one(a_hi, b_hi) + (one(a_lo, b_hi) + one(a_hi, b_lo))


def tree_kernel(near_scale, flags_ref, coef_ref, transfer_ref, coupling_ref, basis_ref, near_ref, out_ref, up0, up1, up2, up3):
    levels = transfer_ref.shape[0]
    group, rhs, rank = coef_ref.shape
    place = lax.axis_index("leaf") % group
    ups = (up0, up1, up2, up3)
    up0[...] = coef_ref[...]
    for t in range(levels - 1):
        count = group >> (t + 1)
        vals = ups[t][...].reshape(count, 2, rhs, rank)
        merged = dot3(vals[:, 0].reshape(count * rhs, rank), transfer_ref[t, 0]) + dot3(
            vals[:, 1].reshape(count * rhs, rank), transfer_ref[t, 1]
        )
        ups[t + 1][...] = merged.reshape(count, rhs, rank)
    coupled = []
    for t in range(levels):
        total = jnp.zeros((rhs, rank), f32)
        for m in range(1, 4):
            flag = flags_ref[0, t, m - 1].astype(f32)
            total = total + flag * dot3(ups[t][(place >> t) ^ m], coupling_ref[t, m - 1])
        coupled.append(total)
    coef = coupled[-1]
    for t in range(levels - 1, 0, -1):
        side = (place >> (t - 1)) & 1
        coef = coupled[t - 1] + dot3(coef, transfer_ref[t - 1, side], True)
    coef = coef.astype(bf16)
    leaves, rows = basis_ref.shape[:2]
    for l in range(leaves):
        far = lax.dot_general(coef, basis_ref[l], (((1,), (1,)), ((), ())), preferred_element_type=f32)
        out_ref[:, l * rows:(l + 1) * rows] = (near_ref[l] * near_scale + far).astype(bf16)


def local(n, charges, points, leaf_basis, transfer, coupling, near_list, couple_flags):
    leaves, rows, rank = leaf_basis.shape
    rhs = charges.shape[0]
    levels = transfer.shape[0]
    neighbours = near_list.shape[1]
    basis_rows = leaf_basis.reshape(leaves * rows, rank)
    first = jnp.dot(charges, basis_rows, preferred_element_type=f32)
    group = 2 ** (levels + 1)
    count = 3 * leaves
    blocks = -(-count // 16)
    packed = jnp.pad(points.reshape(count, rows), ((0, blocks * 16 - count), (0, 0))).reshape(blocks, 16, rows)
    vmem = pl.BlockSpec(memory_space=pltpu.VMEM)
    smem = pl.BlockSpec(memory_space=pltpu.SMEM)
    pairs = leaves * neighbours * rows * rows
    near, coefs = pl.pallas_call(
        functools.partial(near_kernel, n, leaves, neighbours),
        out_shape=(
            jax.ShapeDtypeStruct((leaves, rhs, rows), f32),
            jax.ShapeDtypeStruct((group, rhs, rank), f32),
        ),
        in_specs=[smem, vmem, vmem, vmem],
        out_specs=(vmem, vmem),
        scratch_shapes=[
            pltpu.VMEM((2 * reach + 1, leaves + blocks, 16, rows), bf16),
            pltpu.VMEM((2 * reach + 1, blocks * 16, rows), f32),
            pltpu.VMEM((leaves, rows, 16), bf16),
            pltpu.VMEM((group, rhs, rank), f32),
            pltpu.SemaphoreType.DMA((8 + levels + 1,)),
            pltpu.SemaphoreType.DMA((8 + levels + 1,)),
        ],
        compiler_params=pltpu.CompilerParams(
            collective_id=0, has_side_effects=True, vmem_limit_bytes=40 * 2**20
        ),
        cost_estimate=pl.CostEstimate(flops=pairs * 2 * 300, bytes_accessed=2**20, transcendentals=pairs),
        name="near_field",
    )(near_list, charges, packed, first)
    return pl.pallas_call(
        functools.partial(tree_kernel, 1.0 / math.sqrt(neighbours * rows)),
        out_shape=jax.ShapeDtypeStruct((rhs, leaves * rows), bf16),
        in_specs=[smem] + [vmem] * 5,
        out_specs=vmem,
        scratch_shapes=[pltpu.VMEM((group >> t, rhs, rank), f32) for t in range(levels)],
        compiler_params=pltpu.CompilerParams(vmem_limit_bytes=40 * 2**20),
        name="tree_far_field",
    )(couple_flags, coefs, transfer, coupling, leaf_basis, near)


def solution(mesh):
    return jax.shard_map(
        functools.partial(local, mesh.shape["leaf"]),
        mesh=mesh,
        in_specs=(
            P(None, "leaf"),
            P(None, "leaf"),
            P("leaf", None, None),
            P(),
            P(),
            P("leaf", None),
            P("leaf", None, None),
        ),
        out_specs=P(None, "leaf"),
        check_vma=False,
    )
```

```python
import functools
import math

import jax
import jax.numpy as jnp
from jax import lax
from jax.experimental import pallas as pl
from jax.experimental.pallas import tpu as pltpu
from jax.sharding import PartitionSpec as P

smoothing_sq = 0.01
reach = 4
tile = 256
f32 = jnp.float32
bf16 = jnp.bfloat16
MESH = pl.DeviceIdType.MESH


def split3(v):
    hi = v.astype(bf16).astype(f32)
    rest = v - hi
    mid = rest.astype(bf16).astype(f32)
    return hi, mid, rest - mid


def near_kernel(n, leaves, neighbours, near_ref, charges_ref, points_ref, first_ref, out_ref, all_ref, win, pos, targets, coefs, send_sem, recv_sem):
    me = lax.axis_index("leaf")
    core = me % 2
    sibling = me + 1 - 2 * core
    side = (me // 2) % 2
    beside = me ^ 2
    rows = out_ref.shape[-1]
    leaf_step = 1.0 / (2.0 * reach * leaves)

    def each(off, body):
        @pl.when((me + off >= 0) & (me + off < n))
        def _():
            body()

    barrier = pltpu.get_barrier_semaphore()
    group, rhs, rank = coefs.shape
    steps = int(math.log2(group))
    for partner in [sibling, beside] + [me ^ (1 << t) for t in range(3, steps)]:
        pl.semaphore_signal(barrier, inc=1, device_id=(partner,), device_id_type=MESH)
    for off in (-4, 4):
        each(off, lambda: pl.semaphore_signal(barrier, inc=1, device_id=(me + off,), device_id_type=MESH))

    for l in range(leaves):
        win[reach, l] = charges_ref[:, l * rows:(l + 1) * rows]
    for b in range(points_ref.shape[0]):
        win[reach, leaves + b] = points_ref[b]

    peers = 2 + steps - 3
    for off in (-4, 4):
        peers = peers + jnp.where((me + off >= 0) & (me + off < n), 1, 0)
    place = me % group
    coefs[place] = first_ref[...]
    pl.semaphore_wait(barrier, peers)

    def gather(t, incoming=False):
        start = (place >> t) << t
        if incoming:
            start = start ^ (1 << t)
        return pltpu.make_async_remote_copy(
            src_ref=coefs.at[pl.ds(start, 1 << t)],
            dst_ref=coefs.at[pl.ds(start, 1 << t)],
            send_sem=send_sem.at[8 + t],
            recv_sem=recv_sem.at[8 + t],
            device_id=(me ^ (1 << t),),
            device_id_type=MESH,
        )

    def advance(t):
        gather(t, True).wait_recv()
        if t + 1 < steps:
            gather(t + 1).start()

    gather(0).start()

    def copy(src_slot, dst_slot, sem, target):
        return pltpu.make_async_remote_copy(
            src_ref=win.at[src_slot],
            dst_ref=win.at[dst_slot],
            send_sem=send_sem.at[sem],
            recv_sem=recv_sem.at[sem],
            device_id=(target,),
            device_id_type=MESH,
        )

    direct = {off: copy(reach, reach - off, i, me + off) for i, off in enumerate((4, -4))}
    received = {off: copy(reach, reach + off, i, me - off) for i, off in enumerate((-4, 4))}
    to_sib = [(copy(reach, reach - 1, 4, sibling), core == 0), (copy(reach, reach + 1, 4, sibling), core == 1)]
    from_sib = [(copy(reach, reach + 1, 4, sibling), core == 0), (copy(reach, reach - 1, 4, sibling), core == 1)]

    to_beside = [(copy(reach, reach - 2, 2, beside), side == 0), (copy(reach, reach + 2, 2, beside), side == 1)]
    from_beside = [(copy(reach, reach + 2, 2, beside), side == 0), (copy(reach, reach - 2, 2, beside), side == 1)]
    relay_out = [
        (copy(reach + 4, reach + 2, 3, beside), (side == 0) & (me + 4 < n)),
        (copy(reach - 4, reach - 2, 3, beside), (side == 1) & (me - 4 >= 0)),
    ]
    relay_in = [
        (copy(reach - 4, reach - 2, 3, beside), (side == 0) & (me - 2 >= 0)),
        (copy(reach + 4, reach + 2, 3, beside), (side == 1) & (me + 2 < n)),
    ]

    def when(cond, body):
        @pl.when(cond)
        def _():
            body()

    for off in (4, -4):
        each(off, lambda: direct[off].start())
    for c, cond in to_beside + to_sib:
        when(cond, lambda: c.start())

    forwards = [
        (4, 3, 5, 0), (-4, -3, 5, 1),
        (2, 1, 6, 0), (2, 3, 6, 1),
        (-2, -3, 7, 0), (-2, -1, 7, 1),
    ]

    def fwd(entry, act, arriving, also=True):
        held, there, sem, sender = entry
        if arriving:
            valid = (me + there >= 0) & (me + there < n) & (core == 1 - sender)
        else:
            valid = (me + held >= 0) & (me + held < n) & (core == sender) & also
        c = copy(reach + held, reach + there, sem, sibling)
        when(valid, lambda: act(c))

    def to_float(slot):
        for b in range(points_ref.shape[0]):
            pos[slot, b * 16:(b + 1) * 16, :] = win[slot, leaves + b].astype(f32)

    to_float(reach)
    ones = jnp.ones((1, rows), f32)

    def tail(count):
        return jnp.zeros((count, rows), f32)

    def coords(slot, l):
        return [pos[slot, pl.ds(c * leaves + l, 1), :] for c in range(3)]

    def target(a, carry):
        tx, ty, tz = coords(reach, a)
        feats = jnp.concatenate(
            [-2.0 * tx, -2.0 * ty, -2.0 * tz, tx, *split3(tx * tx + ty * ty + tz * tz), ones, ones, ones, tail(6)],
            axis=0,
        )
        targets[a] = feats.T.astype(bf16)
        return carry

    lax.fori_loop(0, leaves, target, 0)

    def source_features(offset, source):
        sx, sy, sz = source
        shift = offset * leaf_step
        norm = sx * sx + sy * sy + sz * sz + (shift * shift + smoothing_sq) + (2.0 * shift) * sx
        return jnp.concatenate(
            [sx, sy, sz, (-2.0 * shift) * ones, ones, ones, ones, *split3(norm), tail(6)], axis=0
        ).astype(bf16)

    def near_of(a, sources):
        parts = [(s, k) for k in range(len(sources)) for s in range(rows // tile)]
        feats = [source_features(offset, source) for offset, source, vals in sources]

        def distances(s, k):
            return jnp.dot(targets[a], feats[k][:, s * tile:(s + 1) * tile], preferred_element_type=f32)

        total = None
        dist_sq = distances(*parts[0])
        for i, (s, k) in enumerate(parts):
            later = distances(*parts[i + 1]) if i + 1 < len(parts) else None
            block = lax.rsqrt(dist_sq.astype(bf16))
            product = lax.dot_general(
                block, sources[k][2][:, s * tile:(s + 1) * tile], (((1,), (1,)), ((), ())), preferred_element_type=f32
            )
            total = product if total is None else total + product
            dist_sq = later
        return total.T

    def own_leaf(a, carry):
        out_ref[a] = near_of(a, [(0.0, coords(reach, a), win[reach, a])])
        return carry

    lax.fori_loop(0, leaves, own_leaf, 0)
    advance(0)

    each(4, lambda: received[4].wait_recv())
    each(-4, lambda: received[-4].wait_recv())
    for c, cond in relay_out:
        when(cond, lambda: c.start())
    for entry in forwards[:2]:
        fwd(entry, lambda c: c.start(), False)
    to_float(0)
    to_float(2 * reach)

    def far_leaf(a, carry):
        ahead = near_ref[a, 1] > me * leaves + a
        source = [jnp.where(ahead, x, y) for x, y in zip(coords(2 * reach, a), coords(0, a))]
        vals = jnp.where(ahead, win[2 * reach, a], win[0, a])
        offset = jnp.where(ahead, 1.0, -1.0) * (reach * leaves)
        out_ref[a] += near_of(a, [(offset, source, vals)])
        return carry

    lax.fori_loop(0, leaves // 2, far_leaf, 0)
    advance(1)
    for c, cond in from_beside:
        when(cond, lambda: c.wait_recv())
    for entry in forwards[2:]:
        fwd(entry, lambda c: c.start(), False, side == (0 if entry[0] > 0 else 1))
    lax.fori_loop(leaves // 2, leaves, far_leaf, 0)
    for c, cond in relay_in:
        when(cond, lambda: c.wait_recv())
    for entry in forwards[2:]:
        fwd(entry, lambda c: c.start(), False, side == (1 if entry[0] > 0 else 0))
    advance(2)

    for c, cond in from_sib:
        when(cond, lambda: c.wait_recv())
    for entry in forwards:
        fwd(entry, lambda c: c.wait_recv(), True)
    for slot in range(1, 2 * reach):
        if slot != reach:
            to_float(slot)

    def others(a, carry):
        sources = []
        for k in range(2, neighbours):
            j = near_ref[a, k]
            slot = jnp.clip((j >> int(math.log2(leaves))) - me + reach, 0, 2 * reach)
            l = j & (leaves - 1)
            sources.append(((j - me * leaves - a).astype(f32), coords(slot, l), win[slot, l]))
        out_ref[a] += near_of(a, sources)
        return carry

    lax.fori_loop(0, leaves // 2, others, 0)
    for t in range(3, steps - 1):
        advance(t)
    lax.fori_loop(leaves // 2, leaves, others, 0)
    advance(steps - 1)
    all_ref[...] = coefs[...]
    for t in range(steps):
        gather(t).wait_send()

    for off in (4, -4):
        each(off, lambda: direct[off].wait_send())
    for c, cond in to_beside + relay_out + to_sib:
        when(cond, lambda: c.wait_send())
    for entry in forwards:
        fwd(entry, lambda c: c.wait_send(), False)


def dot3(a, b, transposed=False):
    dims = (((1,), (1 if transposed else 0,)), ((), ()))
    a_hi = a.astype(bf16)
    b_hi = b.astype(bf16)
    a_lo = (a - a_hi.astype(f32)).astype(bf16)
    b_lo = (b - b_hi.astype(f32)).astype(bf16)

    def one(x, y):
        return lax.dot_general(x, y, dims, preferred_element_type=f32)

    return one(a_hi, b_hi) + (one(a_lo, b_hi) + one(a_hi, b_lo))


def tree_kernel(near_scale, flags_ref, coef_ref, transfer_ref, coupling_ref, basis_ref, near_ref, out_ref, up0, up1, up2, up3):
    levels = transfer_ref.shape[0]
    group, rhs, rank = coef_ref.shape
    place = lax.axis_index("leaf") % group
    ups = (up0, up1, up2, up3)
    up0[...] = coef_ref[...]
    for t in range(levels - 1):
        count = group >> (t + 1)
        vals = ups[t][...].reshape(count, 2, rhs, rank)
        merged = dot3(vals[:, 0].reshape(count * rhs, rank), transfer_ref[t, 0]) + dot3(
            vals[:, 1].reshape(count * rhs, rank), transfer_ref[t, 1]
        )
        ups[t + 1][...] = merged.reshape(count, rhs, rank)
    coupled = []
    for t in range(levels):
        total = jnp.zeros((rhs, rank), f32)
        for m in range(1, 4):
            flag = flags_ref[0, t, m - 1].astype(f32)
            total = total + flag * dot3(ups[t][(place >> t) ^ m], coupling_ref[t, m - 1])
        coupled.append(total)
    coef = coupled[-1]
    for t in range(levels - 1, 0, -1):
        side = (place >> (t - 1)) & 1
        coef = coupled[t - 1] + dot3(coef, transfer_ref[t - 1, side], True)
    coef = coef.astype(bf16)
    leaves, rows = basis_ref.shape[:2]
    for l in range(leaves):
        far = lax.dot_general(coef, basis_ref[l], (((1,), (1,)), ((), ())), preferred_element_type=f32)
        out_ref[:, l * rows:(l + 1) * rows] = (near_ref[l] * near_scale + far).astype(bf16)


def local(n, charges, points, leaf_basis, transfer, coupling, near_list, couple_flags):
    leaves, rows, rank = leaf_basis.shape
    rhs = charges.shape[0]
    levels = transfer.shape[0]
    neighbours = near_list.shape[1]
    basis_rows = leaf_basis.reshape(leaves * rows, rank)
    first = jnp.dot(charges, basis_rows, preferred_element_type=f32)
    group = 2 ** (levels + 1)
    count = 3 * leaves
    blocks = -(-count // 16)
    packed = jnp.pad(points.reshape(count, rows), ((0, blocks * 16 - count), (0, 0))).reshape(blocks, 16, rows)
    vmem = pl.BlockSpec(memory_space=pltpu.VMEM)
    smem = pl.BlockSpec(memory_space=pltpu.SMEM)
    pairs = leaves * neighbours * rows * rows
    near, coefs = pl.pallas_call(
        functools.partial(near_kernel, n, leaves, neighbours),
        out_shape=(
            jax.ShapeDtypeStruct((leaves, rhs, rows), f32),
            jax.ShapeDtypeStruct((group, rhs, rank), f32),
        ),
        in_specs=[smem, vmem, vmem, vmem],
        out_specs=(vmem, vmem),
        scratch_shapes=[
            pltpu.VMEM((2 * reach + 1, leaves + blocks, 16, rows), bf16),
            pltpu.VMEM((2 * reach + 1, blocks * 16, rows), f32),
            pltpu.VMEM((leaves, rows, 16), bf16),
            pltpu.VMEM((group, rhs, rank), f32),
            pltpu.SemaphoreType.DMA((8 + levels + 1,)),
            pltpu.SemaphoreType.DMA((8 + levels + 1,)),
        ],
        compiler_params=pltpu.CompilerParams(
            collective_id=0, has_side_effects=True, vmem_limit_bytes=40 * 2**20
        ),
        cost_estimate=pl.CostEstimate(flops=pairs * 2 * 300, bytes_accessed=2**20, transcendentals=pairs),
        name="near_field",
    )(near_list, charges, packed, first)
    return pl.pallas_call(
        functools.partial(tree_kernel, 1.0 / math.sqrt(neighbours * rows)),
        out_shape=jax.ShapeDtypeStruct((rhs, leaves * rows), bf16),
        in_specs=[smem] + [vmem] * 5,
        out_specs=vmem,
        scratch_shapes=[pltpu.VMEM((group >> t, rhs, rank), f32) for t in range(levels)],
        compiler_params=pltpu.CompilerParams(vmem_limit_bytes=40 * 2**20),
        name="tree_far_field",
    )(couple_flags, coefs, transfer, coupling, leaf_basis, near)


def solution(mesh):
    return jax.shard_map(
        functools.partial(local, mesh.shape["leaf"]),
        mesh=mesh,
        in_specs=(
            P(None, "leaf"),
            P(None, "leaf"),
            P("leaf", None, None),
            P(),
            P(),
            P("leaf", None),
            P("leaf", None, None),
        ),
        out_specs=P(None, "leaf"),
        check_vma=False,
    )
```

```python
import functools
import math

import jax
import jax.numpy as jnp
from jax import lax
from jax.experimental import pallas as pl
from jax.experimental.pallas import tpu as pltpu
from jax.sharding import PartitionSpec as P

smoothing_sq = 0.01
reach = 4
tile = 512
f32 = jnp.float32
bf16 = jnp.bfloat16
MESH = pl.DeviceIdType.MESH


def split3(v):
    hi = v.astype(bf16).astype(f32)
    rest = v - hi
    mid = rest.astype(bf16).astype(f32)
    return hi, mid, rest - mid


def near_kernel(n, leaves, neighbours, near_ref, charges_ref, points_ref, first_ref, out_ref, all_ref, win, pos, targets, coefs, send_sem, recv_sem):
    me = lax.axis_index("leaf")
    core = me % 2
    sibling = me + 1 - 2 * core
    side = (me // 2) % 2
    beside = me ^ 2
    rows = out_ref.shape[-1]
    leaf_step = 1.0 / (2.0 * reach * leaves)

    def each(off, body):
        @pl.when((me + off >= 0) & (me + off < n))
        def _():
            body()

    barrier = pltpu.get_barrier_semaphore()
    group, rhs, rank = coefs.shape
    steps = int(math.log2(group))
    for partner in [sibling, beside] + [me ^ (1 << t) for t in range(3, steps)]:
        pl.semaphore_signal(barrier, inc=1, device_id=(partner,), device_id_type=MESH)
    for off in (-4, 4):
        each(off, lambda: pl.semaphore_signal(barrier, inc=1, device_id=(me + off,), device_id_type=MESH))

    for l in range(leaves):
        win[reach, l] = charges_ref[:, l * rows:(l + 1) * rows]
    for b in range(points_ref.shape[0]):
        win[reach, leaves + b] = points_ref[b]

    peers = 2 + steps - 3
    for off in (-4, 4):
        peers = peers + jnp.where((me + off >= 0) & (me + off < n), 1, 0)
    place = me % group
    coefs[place] = first_ref[...]
    pl.semaphore_wait(barrier, peers)

    def gather(t, incoming=False):
        start = (place >> t) << t
        if incoming:
            start = start ^ (1 << t)
        return pltpu.make_async_remote_copy(
            src_ref=coefs.at[pl.ds(start, 1 << t)],
            dst_ref=coefs.at[pl.ds(start, 1 << t)],
            send_sem=send_sem.at[8 + t],
            recv_sem=recv_sem.at[8 + t],
            device_id=(me ^ (1 << t),),
            device_id_type=MESH,
        )

    def advance(t):
        gather(t, True).wait_recv()
        if t + 1 < steps:
            gather(t + 1).start()

    gather(0).start()

    def copy(src_slot, dst_slot, sem, target):
        return pltpu.make_async_remote_copy(
            src_ref=win.at[src_slot],
            dst_ref=win.at[dst_slot],
            send_sem=send_sem.at[sem],
            recv_sem=recv_sem.at[sem],
            device_id=(target,),
            device_id_type=MESH,
        )

    direct = {off: copy(reach, reach - off, i, me + off) for i, off in enumerate((4, -4))}
    received = {off: copy(reach, reach + off, i, me - off) for i, off in enumerate((-4, 4))}
    to_sib = [(copy(reach, reach - 1, 4, sibling), core == 0), (copy(reach, reach + 1, 4, sibling), core == 1)]
    from_sib = [(copy(reach, reach + 1, 4, sibling), core == 0), (copy(reach, reach - 1, 4, sibling), core == 1)]

    to_beside = [(copy(reach, reach - 2, 2, beside), side == 0), (copy(reach, reach + 2, 2, beside), side == 1)]
    from_beside = [(copy(reach, reach + 2, 2, beside), side == 0), (copy(reach, reach - 2, 2, beside), side == 1)]
    relay_out = [
        (copy(reach + 4, reach + 2, 3, beside), (side == 0) & (me + 4 < n)),
        (copy(reach - 4, reach - 2, 3, beside), (side == 1) & (me - 4 >= 0)),
    ]
    relay_in = [
        (copy(reach - 4, reach - 2, 3, beside), (side == 0) & (me - 2 >= 0)),
        (copy(reach + 4, reach + 2, 3, beside), (side == 1) & (me + 2 < n)),
    ]

    def when(cond, body):
        @pl.when(cond)
        def _():
            body()

    for off in (4, -4):
        each(off, lambda: direct[off].start())
    for c, cond in to_beside + to_sib:
        when(cond, lambda: c.start())

    forwards = [
        (4, 3, 5, 0), (-4, -3, 5, 1),
        (2, 1, 6, 0), (2, 3, 6, 1),
        (-2, -3, 7, 0), (-2, -1, 7, 1),
    ]

    def fwd(entry, act, arriving, also=True):
        held, there, sem, sender = entry
        if arriving:
            valid = (me + there >= 0) & (me + there < n) & (core == 1 - sender)
        else:
            valid = (me + held >= 0) & (me + held < n) & (core == sender) & also
        c = copy(reach + held, reach + there, sem, sibling)
        when(valid, lambda: act(c))

    def to_float(slot):
        for b in range(points_ref.shape[0]):
            pos[slot, b * 16:(b + 1) * 16, :] = win[slot, leaves + b].astype(f32)

    to_float(reach)
    ones = jnp.ones((1, rows), f32)

    def tail(count):
        return jnp.zeros((count, rows), f32)

    def coords(slot, l):
        return [pos[slot, pl.ds(c * leaves + l, 1), :] for c in range(3)]

    def target(a, carry):
        tx, ty, tz = coords(reach, a)
        feats = jnp.concatenate(
            [-2.0 * tx, -2.0 * ty, -2.0 * tz, tx, *split3(tx * tx + ty * ty + tz * tz), ones, ones, ones, tail(6)],
            axis=0,
        )
        targets[a] = feats.T.astype(bf16)
        return carry

    lax.fori_loop(0, leaves, target, 0)

    def source_features(offset, source):
        sx, sy, sz = source
        shift = offset * leaf_step
        norm = sx * sx + sy * sy + sz * sz + (shift * shift + smoothing_sq) + (2.0 * shift) * sx
        return jnp.concatenate(
            [sx, sy, sz, (-2.0 * shift) * ones, ones, ones, ones, *split3(norm), tail(6)], axis=0
        ).astype(bf16)

    def near_of(a, sources):
        parts = [(s, k) for k in range(len(sources)) for s in range(rows // tile)]
        feats = [source_features(offset, source) for offset, source, vals in sources]

        def distances(s, k):
            return jnp.dot(targets[a], feats[k][:, s * tile:(s + 1) * tile], preferred_element_type=f32)

        total = None
        dist_sq = distances(*parts[0])
        for i, (s, k) in enumerate(parts):
            later = distances(*parts[i + 1]) if i + 1 < len(parts) else None
            block = lax.rsqrt(dist_sq.astype(bf16))
            product = lax.dot_general(
                block, sources[k][2][:, s * tile:(s + 1) * tile], (((1,), (1,)), ((), ())), preferred_element_type=f32
            )
            total = product if total is None else total + product
            dist_sq = later
        return total.T

    def own_leaf(a, carry):
        out_ref[a] = near_of(a, [(0.0, coords(reach, a), win[reach, a])])
        return carry

    lax.fori_loop(0, leaves, own_leaf, 0)
    advance(0)

    each(4, lambda: received[4].wait_recv())
    each(-4, lambda: received[-4].wait_recv())
    for c, cond in relay_out:
        when(cond, lambda: c.start())
    for entry in forwards[:2]:
        fwd(entry, lambda c: c.start(), False)
    to_float(0)
    to_float(2 * reach)

    def far_leaf(a, carry):
        ahead = near_ref[a, 1] > me * leaves + a
        source = [jnp.where(ahead, x, y) for x, y in zip(coords(2 * reach, a), coords(0, a))]
        vals = jnp.where(ahead, win[2 * reach, a], win[0, a])
        offset = jnp.where(ahead, 1.0, -1.0) * (reach * leaves)
        out_ref[a] += near_of(a, [(offset, source, vals)])
        return carry

    lax.fori_loop(0, leaves // 2, far_leaf, 0)
    advance(1)
    for c, cond in from_beside:
        when(cond, lambda: c.wait_recv())
    for entry in forwards[2:]:
        fwd(entry, lambda c: c.start(), False, side == (0 if entry[0] > 0 else 1))
    lax.fori_loop(leaves // 2, leaves, far_leaf, 0)
    for c, cond in relay_in:
        when(cond, lambda: c.wait_recv())
    for entry in forwards[2:]:
        fwd(entry, lambda c: c.start(), False, side == (1 if entry[0] > 0 else 0))
    advance(2)

    for c, cond in from_sib:
        when(cond, lambda: c.wait_recv())
    for entry in forwards:
        fwd(entry, lambda c: c.wait_recv(), True)
    for slot in range(1, 2 * reach):
        if slot != reach:
            to_float(slot)

    def others(a, carry):
        sources = []
        for k in range(2, neighbours):
            j = near_ref[a, k]
            slot = jnp.clip((j >> int(math.log2(leaves))) - me + reach, 0, 2 * reach)
            l = j & (leaves - 1)
            sources.append(((j - me * leaves - a).astype(f32), coords(slot, l), win[slot, l]))
        out_ref[a] += near_of(a, sources)
        return carry

    lax.fori_loop(0, leaves // 2, others, 0)
    for t in range(3, steps - 1):
        advance(t)
    lax.fori_loop(leaves // 2, leaves, others, 0)
    advance(steps - 1)
    all_ref[...] = coefs[...]
    for t in range(steps):
        gather(t).wait_send()

    for off in (4, -4):
        each(off, lambda: direct[off].wait_send())
    for c, cond in to_beside + relay_out + to_sib:
        when(cond, lambda: c.wait_send())
    for entry in forwards:
        fwd(entry, lambda c: c.wait_send(), False)


def dot3(a, b, transposed=False):
    dims = (((1,), (1 if transposed else 0,)), ((), ()))
    a_hi = a.astype(bf16)
    b_hi = b.astype(bf16)
    a_lo = (a - a_hi.astype(f32)).astype(bf16)
    b_lo = (b - b_hi.astype(f32)).astype(bf16)

    def one(x, y):
        return lax.dot_general(x, y, dims, preferred_element_type=f32)

    return one(a_hi, b_hi) + (one(a_lo, b_hi) + one(a_hi, b_lo))


def tree_kernel(near_scale, flags_ref, coef_ref, transfer_ref, coupling_ref, basis_ref, near_ref, out_ref, up0, up1, up2, up3):
    levels = transfer_ref.shape[0]
    group, rhs, rank = coef_ref.shape
    place = lax.axis_index("leaf") % group
    ups = (up0, up1, up2, up3)
    up0[...] = coef_ref[...]
    for t in range(levels - 1):
        count = group >> (t + 1)
        vals = ups[t][...].reshape(count, 2, rhs, rank)
        merged = dot3(vals[:, 0].reshape(count * rhs, rank), transfer_ref[t, 0]) + dot3(
            vals[:, 1].reshape(count * rhs, rank), transfer_ref[t, 1]
        )
        ups[t + 1][...] = merged.reshape(count, rhs, rank)
    coupled = []
    for t in range(levels):
        total = jnp.zeros((rhs, rank), f32)
        for m in range(1, 4):
            flag = flags_ref[0, t, m - 1].astype(f32)
            total = total + flag * dot3(ups[t][(place >> t) ^ m], coupling_ref[t, m - 1])
        coupled.append(total)
    coef = coupled[-1]
    for t in range(levels - 1, 0, -1):
        side = (place >> (t - 1)) & 1
        coef = coupled[t - 1] + dot3(coef, transfer_ref[t - 1, side], True)
    coef = coef.astype(bf16)
    leaves, rows = basis_ref.shape[:2]
    for l in range(leaves):
        far = lax.dot_general(coef, basis_ref[l], (((1,), (1,)), ((), ())), preferred_element_type=f32)
        out_ref[:, l * rows:(l + 1) * rows] = (near_ref[l] * near_scale + far).astype(bf16)


def local(n, charges, points, leaf_basis, transfer, coupling, near_list, couple_flags):
    leaves, rows, rank = leaf_basis.shape
    rhs = charges.shape[0]
    levels = transfer.shape[0]
    neighbours = near_list.shape[1]
    basis_rows = leaf_basis.reshape(leaves * rows, rank)
    first = jnp.dot(charges, basis_rows, preferred_element_type=f32)
    group = 2 ** (levels + 1)
    count = 3 * leaves
    blocks = -(-count // 16)
    packed = jnp.pad(points.reshape(count, rows), ((0, blocks * 16 - count), (0, 0))).reshape(blocks, 16, rows)
    vmem = pl.BlockSpec(memory_space=pltpu.VMEM)
    smem = pl.BlockSpec(memory_space=pltpu.SMEM)
    pairs = leaves * neighbours * rows * rows
    near, coefs = pl.pallas_call(
        functools.partial(near_kernel, n, leaves, neighbours),
        out_shape=(
            jax.ShapeDtypeStruct((leaves, rhs, rows), f32),
            jax.ShapeDtypeStruct((group, rhs, rank), f32),
        ),
        in_specs=[smem, vmem, vmem, vmem],
        out_specs=(vmem, vmem),
        scratch_shapes=[
            pltpu.VMEM((2 * reach + 1, leaves + blocks, 16, rows), bf16),
            pltpu.VMEM((2 * reach + 1, blocks * 16, rows), f32),
            pltpu.VMEM((leaves, rows, 16), bf16),
            pltpu.VMEM((group, rhs, rank), f32),
            pltpu.SemaphoreType.DMA((8 + levels + 1,)),
            pltpu.SemaphoreType.DMA((8 + levels + 1,)),
        ],
        compiler_params=pltpu.CompilerParams(
            collective_id=0, has_side_effects=True, vmem_limit_bytes=40 * 2**20
        ),
        cost_estimate=pl.CostEstimate(flops=pairs * 2 * 300, bytes_accessed=2**20, transcendentals=pairs),
        name="near_field",
    )(near_list, charges, packed, first)
    return pl.pallas_call(
        functools.partial(tree_kernel, 1.0 / math.sqrt(neighbours * rows)),
        out_shape=jax.ShapeDtypeStruct((rhs, leaves * rows), bf16),
        in_specs=[smem] + [vmem] * 5,
        out_specs=vmem,
        scratch_shapes=[pltpu.VMEM((group >> t, rhs, rank), f32) for t in range(levels)],
        compiler_params=pltpu.CompilerParams(vmem_limit_bytes=40 * 2**20),
        name="tree_far_field",
    )(couple_flags, coefs, transfer, coupling, leaf_basis, near)


def solution(mesh):
    return jax.shard_map(
        functools.partial(local, mesh.shape["leaf"]),
        mesh=mesh,
        in_specs=(
            P(None, "leaf"),
            P(None, "leaf"),
            P("leaf", None, None),
            P(),
            P(),
            P("leaf", None),
            P("leaf", None, None),
        ),
        out_specs=P(None, "leaf"),
        check_vma=False,
    )
```
